512 devices in a mesh: feat: 64 (over y_lo, z, core), grp: 8 (over x, y_hi).
Axes of the slice: x: 4, y: 8 (y_hi: 2, y_lo: 4; y = y_hi * 4 + y_lo), z: 8, core: 2. Of those that a mesh axis runs over, the one named last changes fastest.
Arguments:
- gradients: bfloat16 [8, 16777216], P('grp', 'feat'), may hold values from -6 to 6
- sign_bits: int32 [16777216], P('feat'), may hold values 0 or 1
- kept_rows: int32 [16384], replicated, may hold values from 0 to 16777215, as said below
- queries: bfloat16 [512, 16384], P('grp', 'feat'), may hold values from -0.046875 to 0.046875
Outputs:
- projections: bfloat16 [8, 16384], P('grp', 'feat')
- scores: float32 [8, 512], P('grp', 'feat')
The draws below stay inside these ranges and needn't reach their ends.
Inputs may be any that keep to these rules, and one draw needn't show every extreme that they name: kept_rows[k] lies in [j * 16777216 / 64, (j + 1) * 16777216 / 64) for j = k // (K / 64); entries may repeat.
All inputs are finite; a program needn't handle non-finite values. No bound on the sum of `sign_bits` on one device may be relied on, other than what follows from the above.
Results may differ from the reference program's by a relative error of at most 0.0057.
Values may be sent and summed in bfloat16 or wider, within the bound.
A program may use at most 64 MiB of HBM per device.

```python
import math
import jax
import jax.numpy as jnp
from jax import lax

P_SIZE = 16777216
K = 16384
EX = 8
NQ = 512
N_FEAT = 64


def draw_kept_rows(key, part):
    key = jax.random.fold_in(key, 5)
    local_len = P_SIZE // N_FEAT
    per_device = K // N_FEAT
    offsets = jax.random.randint(key, (K,), 0, local_len, dtype=jnp.int32)
    owners = jnp.arange(K, dtype=jnp.int32) // per_device
    chosen = owners * local_len + offsets
    chosen = chosen.at[0].set(0).at[K - 1].set(P_SIZE - 1)
    return chosen


def set_ends(drawn, key, low, largest):
    shape = drawn.shape
    index_at = [jax.random.randint(jax.random.fold_in(key, axis), (), 0, shape[axis]) for axis in range(len(shape))]
    drawn = drawn.at[tuple(index_at)].set(low)
    longest = shape.index(max(shape))
    index_at[longest] = (index_at[longest] + 1) % shape[longest]
    return drawn.at[tuple(index_at)].set(largest)


def shard_levels(stream_key, dims, split, least, largest):
    def one(axis_at, shards_of):
        draws = jax.random.uniform(jax.random.fold_in(jax.random.fold_in(stream_key, 6), axis_at), (shards_of,), jnp.float32, least / len(split), largest / len(split))
        return jnp.repeat(jnp.exp(draws), dims[axis_at] // shards_of).reshape((-1,) + (1,) * (len(dims) - axis_at - 1))

    gain = one(*split[0])
    for cut in split[1:]:
        gain = gain * one(*cut)
    return gain


def scatter_about(stream_key, extent, deviation, limit, cuts=(), held_as=jnp.bfloat16):
    factor_of = shard_levels(stream_key, extent, cuts, -0.22, 0.18) if cuts else 1.0
    drawn = jax.random.normal(stream_key, extent, jnp.float32) * deviation * factor_of
    return jnp.minimum(jnp.maximum(drawn, -limit), limit).astype(held_as)


def setup_inputs(seed: int = 0) -> dict:
    arg_keys = jax.random.split(jax.random.key(seed), 5)
    return {
        "gradients": scatter_about(arg_keys[0], (EX, P_SIZE), 1.0, 6.0, ((0, 8), (1, 64))),
        "sign_bits": set_ends((jax.random.randint(arg_keys[1], (P_SIZE,), 0, 2) < 1).astype(jnp.int32), jax.random.fold_in(arg_keys[1], 1), 0, 1),
        "kept_rows": draw_kept_rows(jax.random.fold_in(arg_keys[4], 71), 0),
        "queries": scatter_about(arg_keys[3], (NQ, K), K ** -0.5, 0.046875, ((0, 8), (1, 64))),
    }


def parity_sign(first_index, second_index, bit_count):
    common = jnp.bitwise_and(first_index, second_index)
    oddity = jnp.zeros_like(common)
    for bit_pos in range(bit_count):
        oddity = jnp.bitwise_xor(oddity, jnp.bitwise_and(jnp.right_shift(common, bit_pos), 1))
    return (1 - 2 * oddity).astype(jnp.float32)

def hadamard_table(length):
    counter = jnp.arange(length, dtype=jnp.int32)
    return parity_sign(counter[:, None], counter[None, :], max(length.bit_length() - 1, 1))

def reference(gradients, sign_bits, kept_rows, queries):
    local_len = P_SIZE // N_FEAT
    total_bits = local_len.bit_length() - 1
    inner_len = 1 << total_bits // 2
    outer_len = local_len // inner_len
    per_device = K // N_FEAT
    table_inner = hadamard_table(inner_len)
    table_outer = hadamard_table(outer_len)
    owners = jnp.arange(K, dtype=jnp.int32) // per_device
    offsets = (kept_rows - owners * local_len).astype(jnp.int32)
    device_ids = jnp.arange(N_FEAT, dtype=jnp.int32)
    mix_signs = parity_sign(owners[:, None], device_ids[None, :], max(N_FEAT.bit_length() - 1, 1))
    flips = sign_bits == 1

    def project_one(example):
        flipped = jnp.where(flips, -example, example).reshape(N_FEAT, outer_len, inner_len)
        section_one = (jnp.einsum('fab,cb->fac', flipped.astype(jnp.float32), table_inner) / math.sqrt(inner_len)).astype(jnp.bfloat16)
        section_two = (jnp.einsum('fab,ca->fcb', section_one.astype(jnp.float32), table_outer) / math.sqrt(outer_len)).astype(jnp.bfloat16)
        picked = section_two.reshape(N_FEAT, local_len)[:, offsets].astype(jnp.float32)
        return (lax.optimization_barrier(jnp.sum(picked.T * mix_signs, axis=1)) / math.sqrt(N_FEAT)).astype(jnp.bfloat16)
    projections = lax.map(project_one, gradients)
    scores = jnp.dot(projections, queries.T, preferred_element_type=jnp.float32)
    return (projections, scores)
```

```python
import functools
import math

import jax
import jax.numpy as jnp
from jax import lax
from jax.experimental import pallas as pl
from jax.experimental.pallas import tpu as pltpu
from jax.sharding import PartitionSpec as P

LANES = 128
PARTS = 4


def sign_of(bits, width):
    shift = 1
    while shift < width:
        shift *= 2
    while shift > 1:
        shift //= 2
        bits = bits ^ (bits >> shift)
    return 1 - 2 * (bits & 1)


def flip_signs(rows, grad_ref, sign_ref, x_ref):
    step = min(rows, 128)
    for part in range(PARTS):
        for block in range(rows // step):
            row = part * rows + block * step
            values = grad_ref[:, pl.ds(row * LANES, step * LANES)].astype(jnp.float32)
            values = values.reshape(step, LANES)
            flips = sign_ref[pl.ds(row, step), :]
            values = jnp.where(flips == 1, -values, values)
            x_ref[pl.ds(block * step, step), pl.ds(part * LANES, LANES)] = values.astype(jnp.bfloat16)


def picked(rows, kept, x):
    picks = kept.shape[1]
    row_bits = rows.bit_length() - 1
    lane_index = kept & (LANES - 1)
    row_index = (kept >> 7) & (rows - 1)
    part_index = (kept >> (7 + row_bits)) & (PARTS - 1)
    step16 = lax.broadcasted_iota(jnp.int32, (16, picks), 0)
    table = sign_of(step16 & lane_index, 4).astype(jnp.float32).astype(jnp.bfloat16)
    bits = [(lane_index >> b) & 1 for b in range(4, 7)] + [part_index & 1, part_index >> 1]
    for bit in bits:
        factor = jnp.broadcast_to((1 - 2 * bit).astype(jnp.float32), (16, picks)).astype(jnp.bfloat16)
        factor = jnp.concatenate([factor] * (table.shape[0] // 16), axis=0)
        table = jnp.concatenate([table, table * factor], axis=0)
    total = jnp.dot(x, table, preferred_element_type=jnp.float32)
    half = rows // 2
    while half >= 8:
        bit = (row_index >> (half.bit_length() - 1)) & 1
        total = total[:half] + total[half:] * (1 - 2 * bit).astype(jnp.float32)
        half //= 2
    step8 = lax.broadcasted_iota(jnp.int32, (8, picks), 0)
    return jnp.sum(total * sign_of(step8 & row_index, 3).astype(jnp.float32), axis=0, keepdims=True)


def kernel(feats, groups, scale, grad_hbm, sign_hbm, kept_ref, query_ref, proj_ref, score_ref,
           grad, sign, x, picks, landed, queries, part, summed,
           load_sem, pick_send, pick_recv, query_send, query_recv, part_send, part_recv):
    feat = lax.axis_index("feat")
    group = lax.axis_index("grp")
    width = picks.shape[2]
    rows = x.shape[0]
    per_owner = score_ref.shape[1]

    load_grad = pltpu.make_async_copy(grad_hbm, grad, load_sem.at[0])
    load_sign = pltpu.make_async_copy(sign_hbm, sign, load_sem.at[1])
    load_grad.start()
    load_sign.start()

    barrier = pltpu.get_barrier_semaphore()

    @pl.loop(1, feats)
    def _(step):
        pl.semaphore_signal(barrier, inc=1, device_id={"feat": lax.rem(feat + step, feats)},
                            device_id_type=pl.DeviceIdType.MESH)

    @pl.loop(1, groups)
    def _(step):
        pl.semaphore_signal(barrier, inc=1, device_id={"grp": lax.rem(group + step, groups)},
                            device_id_type=pl.DeviceIdType.MESH)

    load_grad.wait()
    load_sign.wait()
    flip_signs(rows, grad, sign, x)

    pl.semaphore_wait(barrier, feats + groups - 2)

    @pl.loop(1, groups)
    def _(step):
        pltpu.make_async_remote_copy(
            src_ref=query_ref, dst_ref=queries.at[group],
            send_sem=query_send, recv_sem=query_recv,
            device_id={"grp": lax.rem(group + step, groups)}, device_id_type=pl.DeviceIdType.MESH,
        ).start()

    queries[group] = query_ref[...]

    def block(owner):
        kept = jnp.concatenate(
            [kept_ref[pl.ds(owner * (width // LANES) + i, 1), :] for i in range(width // LANES)], axis=1
        )
        sign_here = sign_of(owner & feat, feats.bit_length() - 1).astype(jnp.float32)
        return picked(rows, kept, x[...]) * (sign_here * scale)

    @pl.loop(1, feats)
    def _(step):
        owner = lax.rem(feat + step, feats)
        picks[owner] = block(owner)
        pltpu.make_async_remote_copy(
            src_ref=picks.at[owner], dst_ref=landed.at[feat],
            send_sem=pick_send, recv_sem=pick_recv,
            device_id={"feat": owner}, device_id_type=pl.DeviceIdType.MESH,
        ).start()

    landed[feat] = block(feat)

    many = picks.at[pl.ds(0, feats - 1)]
    pltpu.make_async_copy(many, many, pick_recv).wait()
    projected = jnp.sum(landed[...], axis=0).astype(jnp.bfloat16)
    proj_ref[...] = projected

    others = queries.at[pl.ds(0, groups - 1)]
    pltpu.make_async_copy(others, others, query_recv).wait()
    every = queries[...].reshape(groups * queries.shape[1], width)
    scores = lax.dot_general(projected, every, (((1,), (1,)), ((), ())), preferred_element_type=jnp.float32)
    for chunk in range(part.shape[0]):
        part[chunk] = scores[:, chunk * LANES:(chunk + 1) * LANES]

    @pl.loop(1, feats)
    def _(step):
        owner = lax.rem(feat + step, feats)
        pltpu.make_async_remote_copy(
            src_ref=part.at[owner * per_owner // LANES], dst_ref=summed.at[feat],
            send_sem=part_send, recv_sem=part_recv,
            device_id={"feat": owner}, device_id_type=pl.DeviceIdType.MESH,
        ).start()

    summed[feat] = part[feat * per_owner // LANES]
    few = summed.at[pl.ds(0, feats - 1)]
    pltpu.make_async_copy(few, few, part_recv).wait()
    total = jnp.sum(summed[...], axis=0)
    shift = LANES - lax.rem(feat * per_owner, LANES)
    total = pltpu.roll(jnp.broadcast_to(total, (8, LANES)), shift, 1)
    score_ref[...] = total[0:1, 0:per_owner]

    pltpu.make_async_copy(many, many, pick_send).wait()
    pltpu.make_async_copy(others, others, query_send).wait()
    pltpu.make_async_copy(few, few, part_send).wait()


def on_device(feats, groups, gradients, sign_bits, kept_rows, queries):
    local_len = sign_bits.shape[0]
    rows = local_len // (PARTS * LANES)
    width = kept_rows.shape[0] // feats
    all_queries = queries.shape[0] * groups
    scale = 1.0 / math.sqrt(local_len * feats)
    vmem = pl.BlockSpec(memory_space=pltpu.VMEM)
    hbm = pl.BlockSpec(memory_space=pl.ANY)
    return pl.pallas_call(
        functools.partial(kernel, feats, groups, scale),
        out_shape=(
            jax.ShapeDtypeStruct((1, width), jnp.bfloat16),
            jax.ShapeDtypeStruct((1, all_queries // feats), jnp.float32),
        ),
        in_specs=[hbm, hbm, vmem, vmem],
        out_specs=(vmem, vmem),
        scratch_shapes=[
            pltpu.VMEM((1, local_len), jnp.bfloat16),
            pltpu.VMEM((local_len // LANES, LANES), jnp.int32),
            pltpu.VMEM((rows, PARTS * LANES), jnp.bfloat16),
            pltpu.VMEM((feats, 1, width), jnp.float32),
            pltpu.VMEM((feats, 1, width), jnp.float32),
            pltpu.VMEM((groups, queries.shape[0], width), jnp.bfloat16),
            pltpu.VMEM((all_queries // LANES, 1, LANES), jnp.float32),
            pltpu.VMEM((feats, 1, LANES), jnp.float32),
            pltpu.SemaphoreType.DMA((2,)),
            pltpu.SemaphoreType.DMA,
            pltpu.SemaphoreType.DMA,
            pltpu.SemaphoreType.DMA,
            pltpu.SemaphoreType.DMA,
            pltpu.SemaphoreType.DMA,
            pltpu.SemaphoreType.DMA,
        ],
        compiler_params=pltpu.CompilerParams(
            collective_id=0, has_side_effects=True, vmem_limit_bytes=48 * 1024 * 1024
        ),
    )(gradients, sign_bits.reshape(local_len // LANES, LANES), kept_rows.reshape(-1, LANES), queries)


def solution(mesh):
    feats, groups = mesh.shape["feat"], mesh.shape["grp"]
    in_specs = (P("grp", "feat"), P("feat"), P(), P("grp", "feat"))
    out_specs = (P("grp", "feat"), P("grp", "feat"))
    return jax.shard_map(
        functools.partial(on_device, feats, groups), mesh=mesh, in_specs=in_specs, out_specs=out_specs,
        check_vma=False,
    )
```

```python
import functools
import math

import jax
import jax.numpy as jnp
from jax import lax
from jax.experimental import pallas as pl
from jax.experimental.pallas import tpu as pltpu
from jax.sharding import PartitionSpec as P

LANES = 128
PARTS = 4
OWNERS = 8
RELAY_STEP = 4


def sign_of(bits, width):
    shift = 1
    while shift < width:
        shift *= 2
    while shift > 1:
        shift //= 2
        bits = bits ^ (bits >> shift)
    return 1 - 2 * (bits & 1)


def across(step, pairs):
    quarter = max(pairs // 4, 1)
    return lax.rem(step, pairs // quarter) * quarter + step // (pairs // quarter)


def flip_signs(part, rows, grad_ref, sign_ref, flipped_ref):
    step = min(rows, 128)
    for block in range(rows // step):
        row = part * rows + block * step
        values = grad_ref[:, pl.ds(row * LANES, step * LANES)].astype(jnp.float32)
        values = values.reshape(step, LANES)
        flips = sign_ref[pl.ds(row, step), :]
        values = jnp.where(flips == 1, -values, values)
        flipped_ref[part, pl.ds(block * step, step), :] = values.astype(jnp.bfloat16)


def picked(rows, kept, x):
    picks = kept.shape[1]
    row_bits = rows.bit_length() - 1
    lane_index = kept & (LANES - 1)
    row_index = (kept >> 7) & (rows - 1)
    part_index = (kept >> (7 + row_bits)) & (PARTS - 1)
    step16 = lax.broadcasted_iota(jnp.int32, (16, picks), 0)
    table = sign_of(step16 & lane_index, 4).astype(jnp.float32).astype(jnp.bfloat16)
    bits = [(lane_index >> b) & 1 for b in range(4, 7)] + [part_index & 1, part_index >> 1]
    for bit in bits:
        factor = jnp.broadcast_to((1 - 2 * bit).astype(jnp.float32), (16, picks)).astype(jnp.bfloat16)
        factor = jnp.concatenate([factor] * (table.shape[0] // 16), axis=0)
        table = jnp.concatenate([table, table * factor], axis=0)
    total = jnp.dot(x, table, preferred_element_type=jnp.float32)
    half = rows // 2
    while half >= 8:
        bit = (row_index >> (half.bit_length() - 1)) & 1
        total = total[:half] + total[half:] * (1 - 2 * bit).astype(jnp.float32)
        half //= 2
    step8 = lax.broadcasted_iota(jnp.int32, (8, picks), 0)
    return jnp.sum(total * sign_of(step8 & row_index, 3).astype(jnp.float32), axis=0, keepdims=True)


def main_kernel(feats, groups, owners, scale, grad_hbm, sign_hbm, kept_hbm, query_hbm, proj_ref, score_ref,
                grad, sign, kept, mine, theirs, x, picks, landed, queries, part, summed, proj, score,
                load_sem, mix_send, mix_recv, pick_send, pick_recv, near_send, near_recv, row_send, row_recv, relay_send, relay_recv,
                store_sem, part_send, part_recv):
    feat = lax.axis_index("feat")
    group = lax.axis_index("grp")
    pairs = feats // 2
    pair = feat // 2
    core = feat & 1
    width = picks.shape[2]
    rows = x.shape[0]
    per_owner = score.shape[1]
    spans = width // LANES
    mesh_ids = pl.DeviceIdType.MESH
    sibling = {"feat": feat ^ 1}
    group_rows = groups // 2

    loads = []
    for p in range(PARTS):
        lanes = pl.ds(p * rows * LANES, rows * LANES)
        span = pl.ds(p * rows, rows)
        loads.append((
            pltpu.make_async_copy(grad_hbm.at[:, lanes], grad.at[:, lanes], load_sem.at[2 * p]),
            pltpu.make_async_copy(sign_hbm.at[span], sign.at[span], load_sem.at[2 * p + 1]),
        ))
    for load_grad, load_sign in loads:
        load_grad.start()
        load_sign.start()
    load_kept = pltpu.make_async_copy(kept_hbm, kept, load_sem.at[2 * PARTS])
    load_query = pltpu.make_async_copy(query_hbm, queries.at[group], load_sem.at[2 * PARTS + 1])
    load_kept.start()
    load_query.start()

    barrier = pltpu.get_barrier_semaphore()
    pl.semaphore_signal(barrier, inc=1, device_id=sibling, device_id_type=mesh_ids)

    pl.semaphore_signal(barrier, inc=1, device_id={"grp": group ^ 1}, device_id_type=mesh_ids)

    @pl.loop(0, pairs)
    def _(step):
        other_pair = pairs - 1 - across(step, pairs)

        @pl.when(other_pair != pair)
        def _():
            pl.semaphore_signal(barrier, inc=1, device_id={"feat": 2 * other_pair + core}, device_id_type=mesh_ids)

    @pl.loop(1, group_rows)
    def _(step):
        pl.semaphore_signal(barrier, inc=1, device_id={"grp": lax.rem(group + 2 * step, groups)},
                            device_id_type=mesh_ids)

    for p, (load_grad, load_sign) in enumerate(loads):
        load_grad.wait()
        load_sign.wait()
        flip_signs(p, rows, grad, sign, mine)
    load_kept.wait()
    load_query.wait()
    pl.semaphore_wait(barrier, pairs + group_rows)

    mixes = [
        pltpu.make_async_remote_copy(
            src_ref=mine.at[p], dst_ref=theirs.at[p], send_sem=mix_send.at[p], recv_sem=mix_recv.at[p],
            device_id=sibling, device_id_type=mesh_ids,
        )
        for p in range(PARTS)
    ]
    for mix in mixes:
        mix.start()
    near = pltpu.make_async_remote_copy(
        src_ref=queries.at[group], dst_ref=queries.at[group], send_sem=near_send, recv_sem=near_recv,
        device_id={"grp": group ^ 1}, device_id_type=mesh_ids,
    )
    near.start()

    @pl.loop(1, group_rows)
    def _(other_row):
        pltpu.make_async_remote_copy(
            src_ref=queries.at[group], dst_ref=queries.at[group], send_sem=row_send, recv_sem=row_recv,
            device_id={"grp": lax.rem(group + 2 * other_row, groups)}, device_id_type=mesh_ids,
        ).start()

    own_sign = (1 - 2 * core).astype(jnp.float32)
    for p, mix in enumerate(mixes):
        mix.wait_recv()
        mixed = theirs[p].astype(jnp.float32) + mine[p].astype(jnp.float32) * own_sign
        x[:, p * LANES:(p + 1) * LANES] = mixed.astype(jnp.bfloat16)

    blocks = pairs // owners
    home = pair // owners

    for step in range(1, blocks + 1):
        first = lax.rem(home + step, blocks) * owners
        rows_kept = jnp.concatenate(
            [kept[pl.ds((2 * (first + i) + core) * spans + j, 1), :] for i in range(owners) for j in range(spans)],
            axis=1,
        )
        values = picked(rows, rows_kept, x[...])
        for i in range(owners):
            owner = first + i
            sign_here = sign_of(owner & pair, max(pairs.bit_length() - 1, 1)).astype(jnp.float32)
            picks[owner] = values[:, i * width:(i + 1) * width] * (sign_here * scale)

        @pl.loop(0, owners)
        def _(i, first=first):
            owner = first + i

            @pl.when(owner != pair)
            def _():
                pltpu.make_async_remote_copy(
                    src_ref=picks.at[owner], dst_ref=landed.at[pair],
                    send_sem=pick_send, recv_sem=pick_recv,
                    device_id={"feat": 2 * owner + core}, device_id_type=mesh_ids,
                ).start()

        if group_rows > 1 and step == min(RELAY_STEP, blocks):
            near.wait_recv()

            @pl.loop(1, group_rows)
            def _(other_row):
                pltpu.make_async_remote_copy(
                    src_ref=queries.at[group ^ 1], dst_ref=queries.at[group ^ 1],
                    send_sem=relay_send, recv_sem=relay_recv,
                    device_id={"grp": lax.rem(group + 2 * other_row, groups)}, device_id_type=mesh_ids,
                ).start()

    if group_rows == 1:
        near.wait_recv()
    landed[pair] = picks[pair]

    many = picks.at[pl.ds(0, pairs - 1)]
    pltpu.make_async_copy(many, many, pick_recv).wait()
    total = jnp.sum(landed[...], axis=0)
    projected = total.astype(jnp.bfloat16)
    proj[...] = projected
    store_proj = pltpu.make_async_copy(proj, proj_ref, store_sem.at[0])
    store_proj.start()
    rest = (total - projected.astype(jnp.float32)).astype(jnp.bfloat16)

    others = queries.at[pl.ds(0, max(group_rows - 1, 1))]
    if group_rows > 1:
        pltpu.make_async_copy(others, others, row_recv).wait()
        pltpu.make_async_copy(others, others, relay_recv).wait()
    every = queries[...].reshape(groups * queries.shape[1], width)
    scores = lax.dot_general(
        jnp.concatenate([projected, rest], axis=0), every, (((1,), (1,)), ((), ())), preferred_element_type=jnp.float32
    )
    scores = scores[0:1] + scores[1:2]
    for chunk in range(part.shape[0]):
        part[chunk] = scores[:, chunk * LANES:(chunk + 1) * LANES]
    @pl.loop(0, feats)
    def _(step):
        owner = 2 * across(step // 2, pairs) + (step & 1)

        @pl.when(owner != feat)
        def _():
            pltpu.make_async_remote_copy(
                src_ref=part.at[owner * per_owner // LANES], dst_ref=summed.at[feat],
                send_sem=part_send, recv_sem=part_recv,
                device_id={"feat": owner}, device_id_type=mesh_ids,
            ).start()

    summed[feat] = part[feat * per_owner // LANES]
    few = summed.at[pl.ds(0, feats - 1)]
    pltpu.make_async_copy(few, few, part_recv).wait()
    total = jnp.sum(summed[...], axis=0)
    shift = LANES - lax.rem(feat * per_owner, LANES)
    total = pltpu.roll(jnp.broadcast_to(total, (8, LANES)), shift, 1)
    score[...] = total[0:1, 0:per_owner]
    store_score = pltpu.make_async_copy(score, score_ref, store_sem.at[1])
    store_score.start()

    pltpu.make_async_copy(many, many, pick_send).wait()
    near.wait_send()
    if group_rows > 1:
        pltpu.make_async_copy(others, others, row_send).wait()
        pltpu.make_async_copy(others, others, relay_send).wait()
    for mix in mixes:
        mix.wait_send()
    pltpu.make_async_copy(few, few, part_send).wait()
    store_proj.wait()
    store_score.wait()


def write_kernel(proj_ref, score_ref, proj_out, score_out, sems):
    copies = [
        pltpu.make_async_copy(proj_ref, proj_out, sems.at[0]),
        pltpu.make_async_copy(score_ref, score_out, sems.at[1]),
    ]
    for copy in copies:
        copy.start()
    for copy in copies:
        copy.wait()


def on_device(feats, groups, gradients, sign_bits, kept_rows, queries):
    local_len = sign_bits.shape[0]
    rows = local_len // (PARTS * LANES)
    width = kept_rows.shape[0] // feats
    pairs = feats // 2
    all_queries = queries.shape[0] * groups
    scale = 1.0 / math.sqrt(local_len * feats)
    hbm = pl.BlockSpec(memory_space=pltpu.HBM)
    dma = pltpu.SemaphoreType.DMA
    outs = (
        jax.ShapeDtypeStruct((1, width), jnp.bfloat16),
        jax.ShapeDtypeStruct((1, all_queries // feats), jnp.float32),
    )
    projections, scores = pl.pallas_call(
        functools.partial(main_kernel, feats, groups, min(OWNERS, pairs), scale),
        out_shape=outs,
        in_specs=[hbm] * 4,
        out_specs=(hbm, hbm),
        scratch_shapes=[
            pltpu.VMEM((1, local_len), jnp.bfloat16),
            pltpu.VMEM((local_len // LANES, LANES), jnp.int32),
            pltpu.VMEM((kept_rows.shape[0] // LANES, LANES), jnp.int32),
            pltpu.VMEM((PARTS, rows, LANES), jnp.bfloat16),
            pltpu.VMEM((PARTS, rows, LANES), jnp.bfloat16),
            pltpu.VMEM((rows, PARTS * LANES), jnp.bfloat16),
            pltpu.VMEM((pairs, 1, width), jnp.float32),
            pltpu.VMEM((pairs, 1, width), jnp.float32),
            pltpu.VMEM((groups, queries.shape[0], width), jnp.bfloat16),
            pltpu.VMEM((all_queries // LANES, 1, LANES), jnp.float32),
            pltpu.VMEM((feats, 1, LANES), jnp.float32),
            pltpu.VMEM((1, width), jnp.bfloat16),
            pltpu.VMEM((1, all_queries // feats), jnp.float32),
            dma((2 * PARTS + 2,)), dma((PARTS,)), dma((PARTS,)), dma, dma, dma, dma, dma, dma, dma, dma, dma((2,)), dma, dma,
        ],
        compiler_params=pltpu.CompilerParams(
            collective_id=0, has_side_effects=True, vmem_limit_bytes=60 * 1024 * 1024
        ),
    )(gradients, sign_bits.reshape(local_len // LANES, LANES), kept_rows.reshape(-1, LANES), queries)
    return pl.pallas_call(
        write_kernel,
        out_shape=outs,
        in_specs=[hbm, hbm],
        out_specs=(hbm, hbm),
        scratch_shapes=[dma((2,))],
        compiler_params=pltpu.CompilerParams(vmem_limit_bytes=60 * 1024 * 1024),
    )(projections, scores)


def solution(mesh):
    feats, groups = mesh.shape["feat"], mesh.shape["grp"]
    in_specs = (P("grp", "feat"), P("feat"), P(), P("grp", "feat"))
    out_specs = (P("grp", "feat"), P("grp", "feat"))
    return jax.shard_map(
        functools.partial(on_device, feats, groups), mesh=mesh, in_specs=in_specs, out_specs=out_specs,
        check_vma=False,
    )
```

```python
import functools
import math

import jax
import jax.numpy as jnp
from jax import lax
from jax.experimental import pallas as pl
from jax.experimental.pallas import tpu as pltpu
from jax.sharding import PartitionSpec as P

LANES = 128
PARTS = 4
OWNERS = 8
ALONE_BLOCKS = 2
MAIN_VMEM = 55196 * 1024


def sign_of(bits, width):
    shift = 1
    while shift < width:
        shift *= 2
    while shift > 1:
        shift //= 2
        bits = bits ^ (bits >> shift)
    return 1 - 2 * (bits & 1)


def across(step, pairs):
    quarter = max(pairs // 4, 1)
    return lax.rem(step, pairs // quarter) * quarter + step // (pairs // quarter)


def flip_signs(part, rows, grad_ref, sign_ref, flipped_ref):
    step = min(rows, 128)
    for block in range(rows // step):
        row = part * rows + block * step
        values = grad_ref[:, pl.ds(row * LANES, step * LANES)].astype(jnp.float32)
        values = values.reshape(step, LANES)
        flips = sign_ref[pl.ds(row, step), :]
        values = jnp.where(flips == 1, -values, values)
        flipped_ref[part, pl.ds(block * step, step), :] = values.astype(jnp.bfloat16)


def picked(rows, kept, x):
    picks = kept.shape[1]
    row_bits = rows.bit_length() - 1
    lane_index = kept & (LANES - 1)
    row_index = (kept >> 7) & (rows - 1)
    part_index = (kept >> (7 + row_bits)) & (PARTS - 1)
    step16 = lax.broadcasted_iota(jnp.int32, (16, picks), 0)
    table = sign_of(step16 & lane_index, 4).astype(jnp.float32).astype(jnp.bfloat16)
    bits = [(lane_index >> b) & 1 for b in range(4, 7)] + [part_index & 1, part_index >> 1]
    for bit in bits:
        factor = jnp.broadcast_to((1 - 2 * bit).astype(jnp.float32), (16, picks)).astype(jnp.bfloat16)
        factor = jnp.concatenate([factor] * (table.shape[0] // 16), axis=0)
        table = jnp.concatenate([table, table * factor], axis=0)
    total = jnp.dot(x, table, preferred_element_type=jnp.float32)
    half = rows // 2
    while half >= 8:
        bit = (row_index >> (half.bit_length() - 1)) & 1
        total = total[:half] + total[half:] * (1 - 2 * bit).astype(jnp.float32)
        half //= 2
    step8 = lax.broadcasted_iota(jnp.int32, (8, picks), 0)
    return jnp.sum(total * sign_of(step8 & row_index, 3).astype(jnp.float32), axis=0, keepdims=True)


def main_kernel(feats, groups, owners, scale, grad_hbm, sign_hbm, kept_hbm, query_hbm, proj_ref, score_ref,
                grad, sign, kept, mine, theirs, x, picks, landed, queries, columns, part, summed,
                load_sem, mix_send, mix_recv, pick_send, pick_recv, cross_send, cross_recv, near_send, near_recv, row_send, row_recv, relay_send, relay_recv,
                part_send, part_recv):
    feat = lax.axis_index("feat")
    group = lax.axis_index("grp")
    pairs = feats // 2
    pair = feat // 2
    core = feat & 1
    width = picks.shape[3]
    rows = x.shape[0]
    per_owner = score_ref.shape[1]
    spans = width // LANES
    mesh_ids = pl.DeviceIdType.MESH
    sibling = {"feat": feat ^ 1}
    group_rows = groups // 2
    length = max(pairs // 4, 1)
    places = sorted(range(length), key=lambda z: -min(z, length - 1 - z))
    everyone = [y * length + z for z in places for y in range(pairs // length)]
    orders = [everyone[i:i + owners] for i in range(0, pairs, owners)]
    alone_blocks = min(ALONE_BLOCKS, len(orders) - 1)
    alone_owners = [owner for order in orders[:alone_blocks] for owner in order]
    in_first = functools.reduce(jnp.logical_or, [pair == owner for owner in alone_owners])
    landed[1] = jnp.zeros_like(landed[1])

    loads = []
    for p in range(PARTS):
        lanes = pl.ds(p * rows * LANES, rows * LANES)
        span = pl.ds(p * rows, rows)
        loads.append((
            pltpu.make_async_copy(grad_hbm.at[:, lanes], grad.at[:, lanes], load_sem.at[2 * p]),
            pltpu.make_async_copy(sign_hbm.at[span], sign.at[span], load_sem.at[2 * p + 1]),
        ))
    for load_grad, load_sign in loads:
        load_grad.start()
        load_sign.start()
    load_kept = pltpu.make_async_copy(kept_hbm, kept, load_sem.at[2 * PARTS])
    load_query = pltpu.make_async_copy(query_hbm, queries.at[group], load_sem.at[2 * PARTS + 1])
    load_kept.start()
    load_query.start()

    barrier = pltpu.get_barrier_semaphore()
    pl.semaphore_signal(barrier, inc=1, device_id=sibling, device_id_type=mesh_ids)

    pl.semaphore_signal(barrier, inc=1, device_id={"grp": group ^ 1}, device_id_type=mesh_ids)

    @pl.loop(0, pairs)
    def _(step):
        other_pair = across(step, pairs)

        @pl.when(other_pair != pair)
        def _():
            pl.semaphore_signal(barrier, inc=1, device_id={"feat": 2 * other_pair + core}, device_id_type=mesh_ids)

    @pl.loop(1, group_rows)
    def _(step):
        pl.semaphore_signal(barrier, inc=1, device_id={"grp": lax.rem(group + 2 * step, groups)},
                            device_id_type=mesh_ids)

    for p, (load_grad, load_sign) in enumerate(loads):
        load_grad.wait()
        load_sign.wait()
        flip_signs(p, rows, grad, sign, mine)
    load_kept.wait()
    load_query.wait()

    def compute(order, table, side, unmixed):
        owner_core = core ^ side
        rows_kept = jnp.concatenate(
            [kept[pl.ds((2 * owner + owner_core) * spans + j, 1), :] for owner in order for j in range(spans)], axis=1
        )
        values = picked(rows, rows_kept, table)
        pair_bits = max(pairs.bit_length() - 1, 1)
        for i, owner in enumerate(order):
            factor = sign_of(owner & pair, pair_bits).astype(jnp.float32) * scale
            if unmixed:
                factor = factor * (1 - 2 * (core & owner_core)).astype(jnp.float32)
            picks[side, owner] = values[:, i * width:(i + 1) * width] * factor

    def send_own(order):
        for owner in order:
            @pl.when(owner != pair)
            def _(owner=owner):
                pltpu.make_async_remote_copy(
                    src_ref=picks.at[0, owner], dst_ref=landed.at[0, pair], send_sem=pick_send, recv_sem=pick_recv,
                    device_id={"feat": 2 * owner + core}, device_id_type=mesh_ids,
                ).start()

    def relay():
        near.wait_recv()

        @pl.loop(1, group_rows)
        def _(other_row):
            pltpu.make_async_remote_copy(
                src_ref=queries.at[group ^ 1], dst_ref=queries.at[group ^ 1],
                send_sem=relay_send, recv_sem=relay_recv,
                device_id={"grp": lax.rem(group + 2 * other_row, groups)}, device_id_type=mesh_ids,
            ).start()

    mixes = [
        pltpu.make_async_remote_copy(
            src_ref=mine.at[p], dst_ref=theirs.at[p], send_sem=mix_send.at[p], recv_sem=mix_recv.at[p],
            device_id=sibling, device_id_type=mesh_ids,
        )
        for p in range(PARTS)
    ]
    near = pltpu.make_async_remote_copy(
        src_ref=queries.at[group], dst_ref=queries.at[group], send_sem=near_send, recv_sem=near_recv,
        device_id={"grp": group ^ 1}, device_id_type=mesh_ids,
    )

    def open_links():
        pl.semaphore_wait(barrier, pairs + group_rows)
        near.start()
        for mix in mixes:
            mix.start()

        @pl.loop(1, group_rows)
        def _(other_row):
            pltpu.make_async_remote_copy(
                src_ref=queries.at[group], dst_ref=queries.at[group], send_sem=row_send, recv_sem=row_recv,
                device_id={"grp": lax.rem(group + 2 * other_row, groups)}, device_id_type=mesh_ids,
            ).start()

    alone = jnp.concatenate([mine[p] for p in range(PARTS)], axis=1)
    far_half = lax.rem(pair, length) >= length // 2
    for step, order in enumerate(orders[:alone_blocks]):
        compute(order, alone, 0, True)
        compute(order, alone, 1, True)
        if step == 0:
            pl.when(far_half)(open_links)
    pl.when(jnp.logical_not(far_half))(open_links)
    for order in orders[:alone_blocks]:
        send_own(order)
    own_sign = (1 - 2 * core).astype(jnp.float32)
    for p, mix in enumerate(mixes):
        mix.wait_recv()
        mixed = theirs[p].astype(jnp.float32) + mine[p].astype(jnp.float32) * own_sign
        x[:, p * LANES:(p + 1) * LANES] = mixed.astype(jnp.bfloat16)

    for owner in alone_owners:
        pltpu.make_async_remote_copy(
            src_ref=picks.at[1, owner], dst_ref=landed.at[1, pair], send_sem=cross_send, recv_sem=cross_recv,
            device_id={"feat": 2 * owner + 1 - core}, device_id_type=mesh_ids,
        ).start()

    for step, order in enumerate(orders[alone_blocks:]):
        compute(order, x[...], 0, False)
        send_own(order)

    landed[0, pair] = picks[0, pair]

    def lay_out(side):
        blocks = [queries[2 * row + side] for row in range(group_rows)]
        return jnp.concatenate(blocks, axis=0).astype(jnp.float32).T.astype(jnp.bfloat16)

    side = group & 1
    others = queries.at[pl.ds(0, max(group_rows - 1, 1))]

    def take_own_side():
        if group_rows > 1:
            pltpu.make_async_copy(others, others, row_recv).wait()

    def take_other_side():
        if group_rows > 1:
            pltpu.make_async_copy(others, others, relay_recv).wait()

    relay()
    pl.when(side == 0)(take_own_side)
    pl.when(side == 1)(take_other_side)
    columns[...] = lay_out(0)

    many = picks.at[0, pl.ds(0, pairs - 1)]
    crossed = picks.at[0]
    pltpu.make_async_copy(many, many, pick_recv).wait()

    @pl.when(in_first)
    def _():
        pltpu.make_async_copy(crossed, crossed, cross_recv).wait()

    total = jnp.sum(landed[0] + landed[1], axis=0)
    projected = total.astype(jnp.bfloat16)
    proj_ref[...] = projected
    rest = (total - projected.astype(jnp.float32)).astype(jnp.bfloat16)
    both = jnp.concatenate([projected, rest], axis=0)
    per_group = queries.shape[1] // per_owner

    def place(owner):
        return owner // (2 * per_group) * queries.shape[1] + lax.rem(owner, per_group) * per_owner

    def send_scores(turn, query_side):
        scores = jnp.dot(both, columns[...], preferred_element_type=jnp.float32)
        scores = scores[0:1] + scores[1:2]
        for chunk in range(part.shape[1]):
            part[turn, chunk] = scores[:, chunk * LANES:(chunk + 1) * LANES]

        @pl.loop(0, feats)
        def _(step):
            owner = 2 * across(step // 2, pairs) + (step & 1)
            on_side = (owner // per_group) & 1 == query_side

            @pl.when(jnp.logical_and(on_side, owner != feat))
            def _():
                pltpu.make_async_remote_copy(
                    src_ref=part.at[turn, place(owner) // LANES], dst_ref=summed.at[feat],
                    send_sem=part_send, recv_sem=part_recv,
                    device_id={"feat": owner}, device_id_type=mesh_ids,
                ).start()

            @pl.when(jnp.logical_and(on_side, owner == feat))
            def _():
                summed[feat] = part[turn, place(owner) // LANES]

    send_scores(0, 0)
    pl.when(side == 1)(take_own_side)
    pl.when(side == 0)(take_other_side)
    columns[...] = lay_out(1)
    send_scores(1, 1)

    few = summed.at[pl.ds(0, feats - 1)]
    pltpu.make_async_copy(few, few, part_recv).wait()
    total = jnp.sum(summed[...], axis=0)
    shift = LANES - lax.rem(place(feat), LANES)
    total = pltpu.roll(jnp.broadcast_to(total, (8, LANES)), shift, 1)
    score_ref[...] = total[0:1, 0:per_owner]

    pltpu.make_async_copy(many, many, pick_send).wait()
    gone = picks.at[0, pl.ds(0, len(alone_owners))]
    pltpu.make_async_copy(gone, gone, cross_send).wait()
    near.wait_send()
    if group_rows > 1:
        pltpu.make_async_copy(others, others, row_send).wait()
        pltpu.make_async_copy(others, others, relay_send).wait()
    for mix in mixes:
        mix.wait_send()
    pltpu.make_async_copy(few, few, part_send).wait()


def write_kernel(proj_ref, score_ref, proj_out, score_out, sems):
    copies = [
        pltpu.make_async_copy(proj_ref, proj_out, sems.at[0]),
        pltpu.make_async_copy(score_ref, score_out, sems.at[1]),
    ]
    for copy in copies:
        copy.start()
    for copy in copies:
        copy.wait()


def on_device(feats, groups, gradients, sign_bits, kept_rows, queries):
    local_len = sign_bits.shape[0]
    rows = local_len // (PARTS * LANES)
    width = kept_rows.shape[0] // feats
    pairs = feats // 2
    all_queries = queries.shape[0] * groups
    scale = 1.0 / math.sqrt(local_len * feats)
    hbm = pl.BlockSpec(memory_space=pltpu.HBM)
    vmem = pl.BlockSpec(memory_space=pltpu.VMEM)
    dma = pltpu.SemaphoreType.DMA
    outs = (
        jax.ShapeDtypeStruct((1, width), jnp.bfloat16),
        jax.ShapeDtypeStruct((1, all_queries // feats), jnp.float32),
    )
    projections, scores = pl.pallas_call(
        functools.partial(main_kernel, feats, groups, min(OWNERS, pairs // 2), scale),
        out_shape=outs,
        in_specs=[hbm] * 4,
        out_specs=(vmem, vmem),
        scratch_shapes=[
            pltpu.VMEM((1, local_len), jnp.bfloat16),
            pltpu.VMEM((local_len // LANES, LANES), jnp.int32),
            pltpu.VMEM((kept_rows.shape[0] // LANES, LANES), jnp.int32),
            pltpu.VMEM((PARTS, rows, LANES), jnp.bfloat16),
            pltpu.VMEM((PARTS, rows, LANES), jnp.bfloat16),
            pltpu.VMEM((rows, PARTS * LANES), jnp.bfloat16),
            pltpu.VMEM((2, pairs, 1, width), jnp.float32),
            pltpu.VMEM((2, pairs, 1, width), jnp.float32),
            pltpu.VMEM((groups, queries.shape[0], width), jnp.bfloat16),
            pltpu.VMEM((width, all_queries // 2), jnp.bfloat16),
            pltpu.VMEM((2, all_queries // (2 * LANES), 1, LANES), jnp.float32),
            pltpu.VMEM((feats, 1, LANES), jnp.float32),
            dma((2 * PARTS + 2,)), dma((PARTS,)), dma((PARTS,)), dma, dma, dma, dma, dma, dma, dma, dma, dma, dma, dma, dma,
        ],
        compiler_params=pltpu.CompilerParams(
            collective_id=0, has_side_effects=True, vmem_limit_bytes=MAIN_VMEM
        ),
    )(gradients, sign_bits.reshape(local_len // LANES, LANES), kept_rows.reshape(-1, LANES), queries)
    return pl.pallas_call(
        write_kernel,
        out_shape=outs,
        in_specs=[vmem, vmem],
        out_specs=(hbm, hbm),
        scratch_shapes=[dma((2,))],
        compiler_params=pltpu.CompilerParams(vmem_limit_bytes=8 * 1024 * 1024),
    )(projections, scores)


def solution(mesh):
    feats, groups = mesh.shape["feat"], mesh.shape["grp"]
    in_specs = (P("grp", "feat"), P("feat"), P(), P("grp", "feat"))
    out_specs = (P("grp", "feat"), P("grp", "feat"))
    return jax.shard_map(
        functools.partial(on_device, feats, groups), mesh=mesh, in_specs=in_specs, out_specs=out_specs,
        check_vma=False,
    )
```
